32 devices in a mesh: depth: 4 (over z), plane: 8 (over y, x, core).
Axes of the slice: x: 2, y: 2, z: 4, core: 2. Of those that a mesh axis runs over, the one named last changes fastest.
Arguments:
- toar: bfloat16 [4, 8, 2, 16384], P('depth', None, None, 'plane'), may hold values from -6 to 6
- pml_coeff: float32 [4, 2, 16384], P('depth', None, 'plane'), may hold values from -1.5 to 1.5
- coupling: float32 [4, 16384], P('depth', 'plane'), may hold values from 0.5 to 1
- inverse: bfloat16 [4, 256, 16, 64, 128], P('depth', 'plane'), may hold values from -0.125 to 0.125
- pattern: int32 [4, 256, 16], P('depth', 'plane'), may hold values from 0 to 255
- patch_map: int32 [4, 16384], P('depth', 'plane'), may hold values from 0 to 4095, as said below
Outputs:
- precond: bfloat16 [4, 8, 2, 16384], P('depth', None, None, 'plane')
- patch_sens: float32 [8, 4096], P(None, ('depth', 'plane'))
The draws below stay inside these ranges and needn't reach their ends.
Inputs may be any that keep to these rules, and one draw needn't show every extreme that they name: `patch_map`: patch p belongs to owner p // 128. Among the cells of one device (one layer, one block of 2048 cells), at most 128 name patches of any one owner, and in every such block some owner is named exactly 128 times. `pattern`: block columns of the whole layer.
All inputs are finite; a program needn't handle non-finite values.
Results may differ from the reference program's by a relative error of at most 0.018.
Values may be sent and summed in bfloat16 or wider, within the bound.
A program may use at most 128 MiB of HBM per device.

```python
import math
import jax
import jax.numpy as jnp

BLK = 64
KNZ = 16
NV = 8
NB_DEV = 32
PATCH_DEV = 128
LAYERS = 4
NBLK = 256
CELLS = 16384
OWNERS = 32
PATCHES = 4096
CAP = 128


def block_owners(key):
    rows = NB_DEV * BLK
    total = OWNERS * CAP
    key_a, key_b, key_c, key_d = jax.random.split(key, 4)
    owner_list = jnp.arange(total, dtype=jnp.int32) // CAP
    favored = jax.random.randint(key_a, (), 0, OWNERS, dtype=jnp.int32)
    priority = jax.random.permutation(key_b, total).astype(jnp.int32)
    priority = jnp.where(owner_list == favored, priority - total, priority)
    order = jnp.argsort(priority, stable=True)
    picked = owner_list[order[:rows]]
    shuffled = picked[jax.random.permutation(key_c, rows)]
    local = jax.random.randint(key_d, (rows,), 0, PATCH_DEV, dtype=jnp.int32)
    return shuffled * PATCH_DEV + local


def draw_patch_map(key, part):
    keys = jax.random.split(jax.random.fold_in(key, 7), OWNERS)
    maps = jax.vmap(block_owners)(keys)
    return maps.reshape(LAYERS, CELLS).astype(jnp.int32)


def set_ends(entries, rng, low, largest):
    longest = entries.shape.index(max(entries.shape))
    spots = []
    for shift in (0, 1):
        where = [jax.random.randint(jax.random.fold_in(rng, axis), (), 0, length) for axis, length in enumerate(entries.shape)]
        where[longest] = (where[longest] + shift) % entries.shape[longest]
        spots.append(tuple(where))
    return entries.at[spots[0]].set(low).at[spots[1]].set(largest)


def level_of(own_key, dims, cuts, least, largest):
    gain, own = 1.0, jax.random.fold_in(own_key, 6)
    for position, blocks in cuts:
        draws = jnp.exp(jax.random.uniform(jax.random.fold_in(own, position), (blocks,), jnp.float32, least / len(cuts), largest / len(cuts)))
        gain = gain * jnp.repeat(draws, dims[position] // blocks).reshape([-1 if axis == position else 1 for axis in range(len(dims))])
    return gain


def scatter_about(key, extent, scale, limit, pieces=(), kind=jnp.bfloat16):
    loudness = level_of(key, extent, pieces, -0.22, 0.18) if pieces else 1.0
    array = jax.random.normal(key, extent, jnp.float32) * scale * loudness
    return jnp.minimum(jnp.maximum(array, -limit), limit).astype(kind)


def setup_inputs(seed: int = 0) -> dict:
    key_list = jax.random.split(jax.random.key(seed), 7)
    return {
        "toar": scatter_about(key_list[0], (LAYERS, NV, 2, CELLS), 1.0, 6.0, ((0, 4), (3, 8))),
        "pml_coeff": jnp.clip(jax.random.uniform(key_list[1], (LAYERS, 2, CELLS), jnp.float32, -1.5, 1.5) * level_of(key_list[1], (LAYERS, 2, CELLS), ((0, 4), (2, 8)), -0.4, 0.0), -1.5, 1.5),
        "coupling": jnp.clip(jnp.exp(math.log(1.0) - 0.6931472 * jax.random.uniform(key_list[2], (LAYERS, CELLS), jnp.float32) ** level_of(key_list[2], (LAYERS, CELLS), ((0, 4), (1, 8)), -0.2, 0.2)), 0.5, 1.0),
        "inverse": scatter_about(key_list[3], (LAYERS, NBLK, KNZ, BLK, 2 * BLK), (2 * KNZ * BLK) ** -0.5, 0.125, ((0, 4), (1, 8))),
        "pattern": set_ends(jax.random.randint(key_list[4], (LAYERS, NBLK, KNZ), 0, NBLK), jax.random.fold_in(key_list[4], 1), 0, NBLK - 1).astype(jnp.int32),
        "patch_map": draw_patch_map(jax.random.fold_in(key_list[6], 71), 0),
    }


def apply_layer(vectors, inv_layer, pattern_layer):
    count = vectors.shape[0]
    block_rows = inv_layer.shape[0]
    per_row = inv_layer.shape[1]
    block_cells = inv_layer.shape[2]
    blocks = vectors.astype(jnp.float32).reshape(count, 2, block_rows, block_cells)
    chosen = jnp.take(blocks, pattern_layer.reshape(-1).astype(jnp.int32), axis=2)
    chosen = chosen.reshape(count, 2, block_rows, per_row, block_cells)
    factor = inv_layer.astype(jnp.float32).reshape(block_rows, per_row, block_cells, 2, block_cells)
    partial_value = jnp.einsum('rkiaj,vbrkj->vabri', factor, chosen)
    real_part = partial_value[:, 0, 0] - partial_value[:, 1, 1]
    imag_part = partial_value[:, 0, 1] + partial_value[:, 1, 0]
    return jnp.stack([real_part, imag_part], axis=1).reshape(count, 2, block_rows * block_cells)


def reference(toar, pml_coeff, coupling, inverse, pattern, patch_map):
    layers = toar.shape[0]
    toar_f32 = toar.astype(jnp.float32)
    sources = []
    for layer in range(layers):
        coeff = pml_coeff[layer]
        real_part = coeff[0] * toar_f32[layer, :, 0] - coeff[1] * toar_f32[layer, :, 1]
        imag_part = coeff[0] * toar_f32[layer, :, 1] + coeff[1] * toar_f32[layer, :, 0]
        sources.append(jnp.stack([real_part, imag_part], axis=1))
    swept = []
    for layer in range(layers):
        down_in = sources[layer]
        if layer > 0:
            down_in = down_in + coupling[layer] * swept[layer - 1].astype(jnp.float32)
        result = apply_layer(down_in.astype(jnp.bfloat16), inverse[layer], pattern[layer])
        swept.append(result.astype(jnp.bfloat16))
    precond = [None] * layers
    precond[layers - 1] = swept[layers - 1]
    for layer in range(layers - 2, -1, -1):
        up_in = (coupling[layer + 1] * precond[layer + 1].astype(jnp.float32)).astype(jnp.bfloat16)
        result = swept[layer].astype(jnp.float32) + apply_layer(up_in, inverse[layer], pattern[layer])
        precond[layer] = result.astype(jnp.bfloat16)
    stacked = jnp.stack(precond, axis=0)
    product = stacked.astype(jnp.float32) * toar_f32
    contrib = product[:, :, 0] + product[:, :, 1]
    contrib = jnp.transpose(contrib, (1, 0, 2)).reshape(contrib.shape[1], -1)
    sums = jax.ops.segment_sum(contrib.T, patch_map.reshape(-1).astype(jnp.int32), num_segments=PATCHES)
    return stacked, sums.T
```

```python
import functools

import jax
import jax.numpy as jnp
from jax import lax
from jax.experimental import pallas as pl
from jax.experimental.pallas import tpu as pltpu
from jax.sharding import PartitionSpec as P

PATCH_DEV = 128
CHUNKS = 4
F32 = jnp.float32
BF16 = jnp.bfloat16


def sweep_kernel(
    depths, planes, pairs, chunks, per_row, vecs,
    pat, src, coup, toar, owner, slot, inv_hbm,
    pre, owned,
    inv, xg, xp, zdn, swept, up, lhs, onehot, part, r1, s1, r2,
    isem, gs, gr, zs, zr, us, ur, as_, ar, bs, br,
):
    d = lax.axis_index("depth")
    p = lax.axis_index("plane")
    step = pairs // chunks
    rows = 2 * step
    owners = depths * planes

    def load(c):
        part_rows = pl.ds(c * rows, rows)
        return pltpu.make_async_copy(inv_hbm.at[part_rows], inv.at[part_rows], isem.at[c])

    for c in range(chunks):
        load(c).start()

    barrier = pltpu.get_barrier_semaphore()

    def greet_plane(o, _):
        pl.semaphore_signal(barrier, inc=1, device_id=(d, lax.rem(p + o, planes)),
                            device_id_type=pl.DeviceIdType.MESH)
        return 0

    def greet_depth(o, _):
        pl.semaphore_signal(barrier, inc=1, device_id=(lax.rem(d + o, depths), p),
                            device_id_type=pl.DeviceIdType.MESH)
        return 0

    lax.fori_loop(1, planes, greet_plane, 0)
    lax.fori_loop(1, depths, greet_depth, 0)
    pl.semaphore_wait(barrier, planes + depths - 2)

    def remote(src_ref, dst_ref, send, recv, target):
        return pltpu.make_async_remote_copy(
            src_ref=src_ref, dst_ref=dst_ref, send_sem=send, recv_sem=recv,
            device_id=target, device_id_type=pl.DeviceIdType.MESH)

    def cut(q, c):
        return pl.ds(q * pairs + c * step, step)

    def gather_copy(phase, o, c, q, target):
        block = xg.at[phase, cut(q, c)]
        return remote(block, block, gs.at[phase, o - 1, c], gr.at[phase, o - 1, c], (d, target))

    def down_copy(c):
        here = pl.ds(c * step, step)
        return remote(swept.at[here], zdn.at[here], zs.at[c], zr.at[c], (lax.rem(d + 1, depths), p))

    def up_copy(c):
        return remote(up.at[pl.ds(c * step, step)], xg.at[1, cut(p, c)], us.at[c], ur.at[c],
                      (lax.rem(d + depths - 1, depths), p))

    left = lax.broadcasted_iota(jnp.int32, (vecs, 128), 1) < 64

    def expand(phase, q):
        def one(i, _):
            n = q * pairs + i
            both = xg[phase, n].astype(F32)
            re, im = both[:vecs], both[vecs:]
            re_t, im_t = pltpu.roll(re, 64, 1), pltpu.roll(im, 64, 1)
            xp[2 * n] = jnp.concatenate(
                [jnp.where(left, re, -im_t), jnp.where(left, im, re_t)], 0).astype(BF16)
            xp[2 * n + 1] = jnp.concatenate(
                [jnp.where(left, re_t, -im), jnp.where(left, im_t, re)], 0).astype(BF16)
            return 0

        lax.fori_loop(0, pairs, one, 0, unroll=4)

    def push(phase, c):
        def one(o, _):
            gather_copy(phase, o, c, p, lax.rem(p + o, planes)).start()
            return 0

        lax.fori_loop(1, planes, one, 0)

    def collect(phase):
        expand(phase, p)

        def one(o, _):
            q = lax.rem(p + planes - o, planes)
            for c in range(chunks):
                gather_copy(phase, o, c, q, q).wait_recv()
            expand(phase, q)
            return 0

        lax.fori_loop(1, planes, one, 0)

    def sent(phase):
        def one(o, _):
            for c in range(chunks):
                gather_copy(phase, o, c, p, lax.rem(p + o, planes)).wait_send()
            return 0

        lax.fori_loop(1, planes, one, 0)

    def block_row(r):
        x = jnp.concatenate([xp[pat[r * per_row + k]] for k in range(per_row)], 1)
        w = jnp.concatenate([inv[r, k] for k in range(per_row)], 1)
        return lax.dot_general(x, w, (((1,), (1,)), ((), ())), preferred_element_type=F32)

    def product(i):
        return jnp.concatenate([block_row(2 * i), block_row(2 * i + 1)], 1)

    def send_up(c):
        @pl.when(d > 0)
        def _():
            def one(i, _):
                n = c * step + i
                up[n] = (coup[n] * pre[n].astype(F32)).astype(BF16)
                return 0

            lax.fori_loop(0, step, one, 0)
            up_copy(c).start()

    @pl.when(d == 0)
    def _():
        zdn[...] = jnp.zeros_like(zdn)

    for c in range(chunks):
        @pl.when(d > 0)
        def _():
            down_copy(c).wait_recv()

        def one(i, _):
            n = c * step + i
            xg[0, p * pairs + n] = (src[n] + coup[n] * zdn[n].astype(F32)).astype(BF16)
            return 0

        lax.fori_loop(0, step, one, 0, unroll=True)
        push(0, c)

    lanes = lax.broadcasted_iota(jnp.int32, (PATCH_DEV, onehot.shape[1]), 0)
    onehot[...] = jnp.where(lanes == slot[...], 1.0, 0.0).astype(BF16)

    collect(0)

    def down_chunk(c, _):
        load(c).wait()

        def one(i, _):
            n = c * step + i
            swept[n] = product(n).astype(BF16)
            return 0

        lax.fori_loop(0, step, one, 0)

        @pl.when(d < depths - 1)
        def _():
            down_copy(c).start()

        @pl.when(d == depths - 1)
        def _():
            def keep(i, _):
                pre[c * step + i] = swept[c * step + i]
                return 0

            lax.fori_loop(0, step, keep, 0)
            send_up(c)

        return 0

    lax.fori_loop(0, chunks, down_chunk, 0)

    @pl.when(d < depths - 1)
    def _():
        for c in range(chunks):
            up_copy(c).wait_recv()
            push(1, c)
        collect(1)

        def up_chunk(c, _):
            def one(i, _):
                n = c * step + i
                pre[n] = (swept[n].astype(F32) + product(n)).astype(BF16)
                return 0

            lax.fori_loop(0, step, one, 0)
            send_up(c)
            return 0

        lax.fori_loop(0, chunks, up_chunk, 0)

    terms = []
    for i in range(pairs):
        both = pre[i].astype(F32) * toar[i].astype(F32)
        terms.append(both[:vecs] + both[vecs:])
    contrib = jnp.concatenate(terms, 1)
    named = jnp.broadcast_to(owner[...], contrib.shape)

    def mask(h, _):
        lhs[h] = jnp.concatenate(
            [jnp.where(named == 2 * h, contrib, 0.0), jnp.where(named == 2 * h + 1, contrib, 0.0)],
            0).astype(BF16)
        return 0

    lax.fori_loop(0, owners // 2, mask, 0)
    part[...] = lax.dot_general(
        lhs[...].reshape(owners * vecs, lhs.shape[2]), onehot[...], (((1,), (1,)), ((), ())),
        preferred_element_type=F32).reshape(owners, vecs, PATCH_DEV)

    def first(o):
        t = lax.rem(d + o, depths)
        return remote(part.at[pl.ds(t * planes, planes)], r1.at[o - 1], as_.at[o - 1], ar.at[o - 1], (t, p))

    for o in range(1, depths):
        first(o).start()
    total = part[pl.ds(d * planes, planes)]
    for o in range(1, depths):
        first(o).wait_recv()
        total = total + r1[o - 1]
    s1[...] = total

    def second(o):
        t = lax.rem(p + o, planes)
        return remote(s1.at[t], r2.at[o - 1], bs.at[o - 1], br.at[o - 1], (d, t))

    for o in range(1, planes):
        second(o).start()
    last = s1[p]
    for o in range(1, planes):
        second(o).wait_recv()
        last = last + r2[o - 1]
    owned[...] = last

    sent(0)

    @pl.when(d < depths - 1)
    def _():
        sent(1)
        for c in range(chunks):
            down_copy(c).wait_send()

    @pl.when(d > 0)
    def _():
        for c in range(chunks):
            up_copy(c).wait_send()

    for o in range(1, depths):
        first(o).wait_send()
    for o in range(1, planes):
        second(o).wait_send()


def shards(toar, pml_coeff, coupling, inverse, pattern, patch_map):
    depths, planes = lax.axis_size("depth"), lax.axis_size("plane")
    _, vecs, _, cells = toar.shape
    block_rows, per_row, blk = inverse.shape[1:4]
    pairs = cells // 128
    owners = depths * planes

    def tiles(value):
        return value.reshape(2 * vecs, pairs, 128).transpose(1, 0, 2)

    vectors = toar[0].transpose(1, 0, 2)
    wide = vectors.astype(F32)
    coeff = pml_coeff[0][:, None]
    source = jnp.concatenate(
        [coeff[0] * wide[0] - coeff[1] * wide[1], coeff[0] * wide[1] + coeff[1] * wide[0]], 0)
    patches = patch_map[0][None]
    tile = (pairs, 2 * vecs, 128)
    vmem = pl.BlockSpec(memory_space=pltpu.VMEM)
    dma = pltpu.SemaphoreType.DMA
    pre, owned = pl.pallas_call(
        functools.partial(sweep_kernel, depths, planes, pairs, CHUNKS, per_row, vecs),
        out_shape=(jax.ShapeDtypeStruct(tile, BF16), jax.ShapeDtypeStruct((vecs, PATCH_DEV), F32)),
        in_specs=[pl.BlockSpec(memory_space=pltpu.SMEM)] + [vmem] * 5 + [pl.BlockSpec(memory_space=pl.ANY)],
        out_specs=(vmem, vmem),
        scratch_shapes=[
            pltpu.VMEM((block_rows, per_row, blk, 2 * blk), BF16),
            pltpu.VMEM((2, planes * pairs, 2 * vecs, 128), BF16),
            pltpu.VMEM((planes * block_rows, 2 * vecs, 128), BF16),
            pltpu.VMEM(tile, BF16),
            pltpu.VMEM(tile, BF16),
            pltpu.VMEM(tile, BF16),
            pltpu.VMEM((owners // 2, 2 * vecs, cells), BF16),
            pltpu.VMEM((PATCH_DEV, cells), BF16),
            pltpu.VMEM((owners, vecs, PATCH_DEV), F32),
            pltpu.VMEM((depths - 1, planes, vecs, PATCH_DEV), F32),
            pltpu.VMEM((planes, vecs, PATCH_DEV), F32),
            pltpu.VMEM((planes - 1, vecs, PATCH_DEV), F32),
            dma((CHUNKS,)),
            dma((2, planes - 1, CHUNKS)),
            dma((2, planes - 1, CHUNKS)),
            dma((CHUNKS,)),
            dma((CHUNKS,)),
            dma((CHUNKS,)),
            dma((CHUNKS,)),
            dma((depths - 1,)),
            dma((depths - 1,)),
            dma((planes - 1,)),
            dma((planes - 1,)),
        ],
        compiler_params=pltpu.CompilerParams(
            collective_id=0, has_side_effects=True, vmem_limit_bytes=40 * 1024 * 1024),
        cost_estimate=pl.CostEstimate(
            flops=4 * block_rows * per_row * blk * 2 * blk * 2 * vecs,
            bytes_accessed=2 * block_rows * per_row * blk * 2 * blk, transcendentals=0),
    )(
        pattern[0].reshape(-1), tiles(source), coupling[0].reshape(pairs, 1, 128),
        tiles(vectors), patches // PATCH_DEV, patches % PATCH_DEV, inverse[0],
    )
    precond = pre.transpose(1, 0, 2).reshape(2, vecs, cells).transpose(1, 0, 2)
    return (precond[None], owned)


def solution(mesh):
    return jax.shard_map(
        shards,
        mesh=mesh,
        in_specs=(
            P("depth", None, None, "plane"),
            P("depth", None, "plane"),
            P("depth", "plane"),
            P("depth", "plane", None, None, None),
            P("depth", "plane", None),
            P("depth", "plane"),
        ),
        out_specs=(P("depth", None, None, "plane"), P(None, ("depth", "plane"))),
        check_vma=False,
    )
```

```python
import functools

import jax
import jax.numpy as jnp
from jax import lax
from jax.experimental import pallas as pl
from jax.experimental.pallas import tpu as pltpu
from jax.sharding import PartitionSpec as P

PATCH_DEV = 128
CHUNKS = 4
F32 = jnp.float32
BF16 = jnp.bfloat16


def sweep_kernel(
    depths, planes, pairs, chunks, per_row, vecs,
    pat, src, coup, toar, patch, inv_hbm,
    pre, owned,
    inv, xg, xp, zdn, swept, up, lhs, onehot, part, r1, s1, r2,
    isem, gs, gr, zs, zr, us, ur, as_, ar, bs, br,
):
    d = lax.axis_index("depth")
    p = lax.axis_index("plane")
    step = pairs // chunks
    rows = 2 * step
    owners = depths * planes

    def load(c):
        part_rows = pl.ds(c * rows, rows)
        return pltpu.make_async_copy(inv_hbm.at[part_rows], inv.at[part_rows], isem.at[c])

    for c in range(chunks):
        load(c).start()

    barrier = pltpu.get_barrier_semaphore()

    def greet_plane(o, _):
        pl.semaphore_signal(barrier, inc=1, device_id=(d, lax.rem(p + o, planes)),
                            device_id_type=pl.DeviceIdType.MESH)
        return 0

    def greet_depth(o, _):
        pl.semaphore_signal(barrier, inc=1, device_id=(lax.rem(d + o, depths), p),
                            device_id_type=pl.DeviceIdType.MESH)
        return 0

    lax.fori_loop(1, planes, greet_plane, 0)
    lax.fori_loop(1, depths, greet_depth, 0)
    pl.semaphore_wait(barrier, planes + depths - 2)

    def remote(src_ref, dst_ref, send, recv, target):
        return pltpu.make_async_remote_copy(
            src_ref=src_ref, dst_ref=dst_ref, send_sem=send, recv_sem=recv,
            device_id=target, device_id_type=pl.DeviceIdType.MESH)

    def cut(q, c):
        return pl.ds(q * pairs + c * step, step)

    groups = planes // 2
    group, twin = p // 2, p % 2
    partner = 2 * group + 1 - twin

    def twin_of(j):
        return 2 * lax.rem(group + j, groups) + twin

    def from_twin(j):
        return 2 * lax.rem(group + groups - j, groups) + twin

    def from_partner(j):
        return 2 * lax.rem(group + groups - j, groups) + 1 - twin

    def twin_copy(phase, j, c, q, target):
        block = xg.at[phase, cut(q, c)]
        return remote(block, block, gs.at[phase, j - 1, c], gr.at[phase, j - 1, c], (d, target))

    def partner_copy(phase, j, c, q):
        block = xg.at[phase, cut(q, c)]
        n = groups - 1 + j
        return remote(block, block, gs.at[phase, n, c], gr.at[phase, n, c], (d, partner))

    def down_copy(c):
        here = pl.ds(c * step, step)
        return remote(swept.at[here], zdn.at[here], zs.at[c], zr.at[c], (lax.rem(d + 1, depths), p))

    def up_copy(c):
        return remote(up.at[pl.ds(c * step, step)], xg.at[1, cut(p, c)], us.at[c], ur.at[c],
                      (lax.rem(d + depths - 1, depths), p))

    left = lax.broadcasted_iota(jnp.int32, (vecs, 128), 1) < 64

    def expand(phase, q):
        def one(i, _):
            n = q * pairs + i
            both = xg[phase, n].astype(F32)
            re, im = both[:vecs], both[vecs:]
            re_t, im_t = pltpu.roll(re, 64, 1), pltpu.roll(im, 64, 1)
            xp[2 * n] = jnp.concatenate(
                [jnp.where(left, re, -im_t), jnp.where(left, im, re_t)], 0).astype(BF16)
            xp[2 * n + 1] = jnp.concatenate(
                [jnp.where(left, re_t, -im), jnp.where(left, im_t, re)], 0).astype(BF16)
            return 0

        lax.fori_loop(0, pairs, one, 0, unroll=4)

    def push(phase, c):
        def one(j, _):
            twin_copy(phase, j, c, p, twin_of(j)).start()
            return 0

        lax.fori_loop(1, groups, one, 0)
        partner_copy(phase, 0, c, p).start()

    def collect(phase):
        expand(phase, p)
        for c in range(chunks):
            def hand(j, _):
                q = from_twin(j)
                twin_copy(phase, j, c, q, q).wait_recv()
                partner_copy(phase, j, c, q).start()
                return 0

            lax.fori_loop(1, groups, hand, 0)

        def near(j, _):
            expand(phase, from_twin(j))
            return 0

        lax.fori_loop(1, groups, near, 0)

        def far(j, _):
            q = from_partner(j)
            for c in range(chunks):
                partner_copy(phase, j, c, q).wait_recv()
            expand(phase, q)
            return 0

        lax.fori_loop(0, groups, far, 0)

    def sent(phase):
        def one(j, _):
            for c in range(chunks):
                twin_copy(phase, j, c, p, twin_of(j)).wait_send()
            return 0

        def other(j, _):
            for c in range(chunks):
                partner_copy(phase, j, c, from_twin(j)).wait_send()
            return 0

        lax.fori_loop(1, groups, one, 0)
        lax.fori_loop(0, groups, other, 0)

    left_all = lax.broadcasted_iota(jnp.int32, (2 * vecs, 128), 1) < 64

    def product(i):
        x = jnp.concatenate(
            [jnp.concatenate([xp[pat[(4 * i + m) * per_row + k]] for k in range(per_row)], 1)
             for m in range(4)], 0)
        w = jnp.concatenate([inv[pl.ds(4 * i, 4), k].reshape(256, 128) for k in range(per_row)], 1)
        y = lax.dot_general(x, w, (((1,), (1,)), ((), ())), preferred_element_type=F32)
        n = 2 * vecs
        return (jnp.where(left_all, y[:n, :128], y[n:2 * n, :128]),
                jnp.where(left_all, y[2 * n:3 * n, 128:], y[3 * n:, 128:]))

    def send_up(c):
        @pl.when(d > 0)
        def _():
            def one(i, _):
                n = c * step + i
                up[n] = (coup[n] * pre[n].astype(F32)).astype(BF16)
                return 0

            lax.fori_loop(0, step, one, 0)
            up_copy(c).start()

    @pl.when(d == 0)
    def _():
        zdn[...] = jnp.zeros_like(zdn)

    for c in range(chunks):
        @pl.when(d > 0)
        def _():
            down_copy(c).wait_recv()

        def one(i, _):
            n = c * step + i
            xg[0, p * pairs + n] = (src[n] + coup[n] * zdn[n].astype(F32)).astype(BF16)
            return 0

        lax.fori_loop(0, step, one, 0, unroll=True)
        push(0, c)

    lanes = lax.broadcasted_iota(jnp.int32, (PATCH_DEV, onehot.shape[1]), 0)
    onehot[...] = jnp.where(lanes == patch[...] % PATCH_DEV, 1.0, 0.0).astype(BF16)

    collect(0)

    def down_chunk(c, _):
        load(c).wait()

        def one(i, _):
            n = c * step + 2 * i
            lower, upper = product(c * (step // 2) + i)
            swept[n] = lower.astype(BF16)
            swept[n + 1] = upper.astype(BF16)
            return 0

        lax.fori_loop(0, step // 2, one, 0)

        @pl.when(d < depths - 1)
        def _():
            down_copy(c).start()

        @pl.when(d == depths - 1)
        def _():
            def keep(i, _):
                pre[c * step + i] = swept[c * step + i]
                return 0

            lax.fori_loop(0, step, keep, 0)
            send_up(c)

        return 0

    lax.fori_loop(0, chunks, down_chunk, 0)

    @pl.when(d < depths - 1)
    def _():
        for c in range(chunks):
            up_copy(c).wait_recv()
            push(1, c)
        collect(1)

        def up_chunk(c, _):
            def one(i, _):
                n = c * step + 2 * i
                lower, upper = product(c * (step // 2) + i)
                pre[n] = (swept[n].astype(F32) + lower).astype(BF16)
                pre[n + 1] = (swept[n + 1].astype(F32) + upper).astype(BF16)
                return 0

            lax.fori_loop(0, step // 2, one, 0)
            send_up(c)
            return 0

        lax.fori_loop(0, chunks, up_chunk, 0)

    terms = []
    for i in range(pairs):
        both = pre[i].astype(F32) * toar[i].astype(F32)
        terms.append(both[:vecs] + both[vecs:])
    contrib = jnp.concatenate(terms, 1)
    named = jnp.broadcast_to(patch[...] // PATCH_DEV, contrib.shape)

    def mask(h, _):
        lhs[h] = jnp.concatenate(
            [jnp.where(named == 2 * h, contrib, 0.0), jnp.where(named == 2 * h + 1, contrib, 0.0)],
            0).astype(BF16)
        return 0

    lax.fori_loop(0, owners // 2, mask, 0)
    part[...] = lax.dot_general(
        lhs[...].reshape(owners * vecs, lhs.shape[2]), onehot[...], (((1,), (1,)), ((), ())),
        preferred_element_type=F32).reshape(owners, vecs, PATCH_DEV)

    def first(o):
        t = lax.rem(d + o, depths)
        return remote(part.at[pl.ds(t * planes, planes)], r1.at[o - 1], as_.at[o - 1], ar.at[o - 1], (t, p))

    for o in range(1, depths):
        first(o).start()
    total = part[pl.ds(d * planes, planes)]
    for o in range(1, depths):
        first(o).wait_recv()
        total = total + r1[o - 1]
    s1[...] = total

    def second(o):
        t = lax.rem(p + o, planes)
        return remote(s1.at[t], r2.at[o - 1], bs.at[o - 1], br.at[o - 1], (d, t))

    for o in range(1, planes):
        second(o).start()
    last = s1[p]
    for o in range(1, planes):
        second(o).wait_recv()
        last = last + r2[o - 1]
    owned[...] = last

    sent(0)

    @pl.when(d < depths - 1)
    def _():
        sent(1)
        for c in range(chunks):
            down_copy(c).wait_send()

    @pl.when(d > 0)
    def _():
        for c in range(chunks):
            up_copy(c).wait_send()

    for o in range(1, depths):
        first(o).wait_send()
    for o in range(1, planes):
        second(o).wait_send()


def shards(toar, pml_coeff, coupling, inverse, pattern, patch_map):
    depths, planes = lax.axis_size("depth"), lax.axis_size("plane")
    _, vecs, _, cells = toar.shape
    block_rows, per_row, blk = inverse.shape[1:4]
    pairs = cells // 128
    owners = depths * planes

    def tiles(value):
        return value.reshape(2 * vecs, pairs, 128).transpose(1, 0, 2)

    vectors = toar[0].transpose(1, 0, 2)
    wide = vectors.astype(F32)
    coeff = pml_coeff[0][:, None]
    source = jnp.concatenate(
        [coeff[0] * wide[0] - coeff[1] * wide[1], coeff[0] * wide[1] + coeff[1] * wide[0]], 0)
    tile = (pairs, 2 * vecs, 128)
    vmem = pl.BlockSpec(memory_space=pltpu.VMEM)
    dma = pltpu.SemaphoreType.DMA
    pre, owned = pl.pallas_call(
        functools.partial(sweep_kernel, depths, planes, pairs, CHUNKS, per_row, vecs),
        out_shape=(jax.ShapeDtypeStruct(tile, BF16), jax.ShapeDtypeStruct((vecs, PATCH_DEV), F32)),
        in_specs=[pl.BlockSpec(memory_space=pltpu.SMEM)] + [vmem] * 4 + [pl.BlockSpec(memory_space=pl.ANY)],
        out_specs=(vmem, vmem),
        scratch_shapes=[
            pltpu.VMEM((block_rows, per_row, blk, 2 * blk), BF16),
            pltpu.VMEM((2, planes * pairs, 2 * vecs, 128), BF16),
            pltpu.VMEM((planes * block_rows, 2 * vecs, 128), BF16),
            pltpu.VMEM(tile, BF16),
            pltpu.VMEM(tile, BF16),
            pltpu.VMEM(tile, BF16),
            pltpu.VMEM((owners // 2, 2 * vecs, cells), BF16),
            pltpu.VMEM((PATCH_DEV, cells), BF16),
            pltpu.VMEM((owners, vecs, PATCH_DEV), F32),
            pltpu.VMEM((depths - 1, planes, vecs, PATCH_DEV), F32),
            pltpu.VMEM((planes, vecs, PATCH_DEV), F32),
            pltpu.VMEM((planes - 1, vecs, PATCH_DEV), F32),
            dma((CHUNKS,)),
            dma((2, planes - 1, CHUNKS)),
            dma((2, planes - 1, CHUNKS)),
            dma((CHUNKS,)),
            dma((CHUNKS,)),
            dma((CHUNKS,)),
            dma((CHUNKS,)),
            dma((depths - 1,)),
            dma((depths - 1,)),
            dma((planes - 1,)),
            dma((planes - 1,)),
        ],
        compiler_params=pltpu.CompilerParams(
            collective_id=0, has_side_effects=True, vmem_limit_bytes=56 * 1024 * 1024),
        cost_estimate=pl.CostEstimate(
            flops=4 * block_rows * per_row * blk * 2 * blk * 2 * vecs,
            bytes_accessed=2 * block_rows * per_row * blk * 2 * blk, transcendentals=0),
    )(
        pattern[0].reshape(-1), tiles(source), coupling[0].reshape(pairs, 1, 128),
        tiles(vectors), patch_map, inverse[0],
    )
    precond = pre.transpose(1, 0, 2).reshape(2, vecs, cells).transpose(1, 0, 2)
    return (precond[None], owned)


def solution(mesh):
    return jax.shard_map(
        shards,
        mesh=mesh,
        in_specs=(
            P("depth", None, None, "plane"),
            P("depth", None, "plane"),
            P("depth", "plane"),
            P("depth", "plane", None, None, None),
            P("depth", "plane", None),
            P("depth", "plane"),
        ),
        out_specs=(P("depth", None, None, "plane"), P(None, ("depth", "plane"))),
        check_vma=False,
    )
```

```python
import functools

import jax
import jax.numpy as jnp
from jax import lax
from jax.experimental import pallas as pl
from jax.experimental.pallas import tpu as pltpu
from jax.sharding import PartitionSpec as P

PATCH_DEV = 128
CHUNKS = 4
F32 = jnp.float32
BF16 = jnp.bfloat16


def sweep_kernel(
    depths, planes, pairs, chunks, per_row, vecs,
    pat, src, coup, toar, patch, inv_hbm,
    pre, owned,
    inv, xg, xp, zdn, swept, up, lhs, onehot, part, r1, s1, r2,
    isem, gs, gr, zs, zr, us, ur, as_, ar, bs, br,
):
    d = lax.axis_index("depth")
    p = lax.axis_index("plane")
    step = pairs // chunks
    rows = 2 * step
    owners = depths * planes

    def load(c):
        part_rows = pl.ds(c * rows, rows)
        return pltpu.make_async_copy(inv_hbm.at[part_rows], inv.at[part_rows], isem.at[c])

    for c in range(chunks):
        load(c).start()

    barrier = pltpu.get_barrier_semaphore()

    def greet_plane(o, _):
        pl.semaphore_signal(barrier, inc=1, device_id=(d, lax.rem(p + o, planes)),
                            device_id_type=pl.DeviceIdType.MESH)
        return 0

    def greet_depth(o, _):
        pl.semaphore_signal(barrier, inc=1, device_id=(lax.rem(d + o, depths), p),
                            device_id_type=pl.DeviceIdType.MESH)
        return 0

    lax.fori_loop(1, planes, greet_plane, 0)
    lax.fori_loop(1, depths, greet_depth, 0)
    pl.semaphore_wait(barrier, planes + depths - 2)

    def remote(src_ref, dst_ref, send, recv, target):
        return pltpu.make_async_remote_copy(
            src_ref=src_ref, dst_ref=dst_ref, send_sem=send, recv_sem=recv,
            device_id=target, device_id_type=pl.DeviceIdType.MESH)

    def cut(q, c):
        return pl.ds(q * pairs + c * step, step)

    groups = planes // 2
    group, twin = p // 2, p % 2
    partner = 2 * group + 1 - twin

    def twin_of(j):
        return 2 * lax.rem(group + j, groups) + twin

    def from_twin(j):
        return 2 * lax.rem(group + groups - j, groups) + twin

    def from_partner(j):
        return 2 * lax.rem(group + groups - j, groups) + 1 - twin

    def twin_copy(phase, j, c, q, target):
        block = xg.at[phase, cut(q, c)]
        return remote(block, block, gs.at[phase, j - 1, c], gr.at[phase, j - 1, c], (d, target))

    def partner_copy(phase, j, c, q):
        block = xg.at[phase, cut(q, c)]
        n = groups - 1 + j
        return remote(block, block, gs.at[phase, n, c], gr.at[phase, n, c], (d, partner))

    def down_copy(c):
        here = pl.ds(c * step, step)
        return remote(swept.at[here], zdn.at[here], zs.at[c], zr.at[c], (lax.rem(d + 1, depths), p))

    def up_copy(c):
        return remote(up.at[pl.ds(c * step, step)], xg.at[1, cut(p, c)], us.at[c], ur.at[c],
                      (lax.rem(d + depths - 1, depths), p))

    left = lax.broadcasted_iota(jnp.int32, (pairs // 2, vecs, 128), 2) < 64

    def expand(phase, q):
        half = pairs // 2
        for h in range(2):
            n = q * pairs + h * half
            both = xg[phase, pl.ds(n, half)].astype(F32)
            re, im = both[:, :vecs], both[:, vecs:]
            re_t, im_t = pltpu.roll(re, 64, 2), pltpu.roll(im, 64, 2)
            even = jnp.concatenate([jnp.where(left, re, -im_t), jnp.where(left, im, re_t)], 1)
            odd = jnp.concatenate([jnp.where(left, re_t, -im), jnp.where(left, im_t, re)], 1)
            tiles = jnp.stack([even, odd], 1).reshape(2 * half, 2 * vecs, 128)
            xp[pl.ds(2 * n, 2 * half)] = tiles.astype(BF16)

    def push(phase, c):
        def one(j, _):
            twin_copy(phase, j, c, p, twin_of(j)).start()
            return 0

        lax.fori_loop(1, groups, one, 0)
        partner_copy(phase, 0, c, p).start()

    def collect(phase):
        expand(phase, p)
        for c in range(chunks):
            def hand(j, _):
                q = from_twin(j)
                twin_copy(phase, j, c, q, q).wait_recv()
                partner_copy(phase, j, c, q).start()
                return 0

            lax.fori_loop(1, groups, hand, 0)

        def near(j, _):
            expand(phase, from_twin(j))
            return 0

        lax.fori_loop(1, groups, near, 0)

        def far(j, _):
            q = from_partner(j)
            for c in range(chunks):
                partner_copy(phase, j, c, q).wait_recv()
            expand(phase, q)
            return 0

        lax.fori_loop(0, groups, far, 0)

    def sent(phase):
        def one(j, _):
            for c in range(chunks):
                twin_copy(phase, j, c, p, twin_of(j)).wait_send()
            return 0

        def other(j, _):
            for c in range(chunks):
                partner_copy(phase, j, c, from_twin(j)).wait_send()
            return 0

        lax.fori_loop(1, groups, one, 0)
        lax.fori_loop(0, groups, other, 0)

    left_all = lax.broadcasted_iota(jnp.int32, (2 * vecs, 128), 1) < 64

    def product(i):
        x = jnp.concatenate(
            [jnp.concatenate([xp[pat[(4 * i + m) * per_row + k]] for k in range(per_row)], 1)
             for m in range(4)], 0)
        w = jnp.concatenate([inv[pl.ds(4 * i, 4), k].reshape(256, 128) for k in range(per_row)], 1)
        y = lax.dot_general(x, w, (((1,), (1,)), ((), ())), preferred_element_type=F32)
        n = 2 * vecs
        return (jnp.where(left_all, y[:n, :128], y[n:2 * n, :128]),
                jnp.where(left_all, y[2 * n:3 * n, 128:], y[3 * n:, 128:]))

    def send_up(c):
        @pl.when(d > 0)
        def _():
            def one(i, _):
                n = c * step + i
                up[n] = (coup[n] * pre[n].astype(F32)).astype(BF16)
                return 0

            lax.fori_loop(0, step, one, 0)
            up_copy(c).start()

    @pl.when(d == 0)
    def _():
        zdn[...] = jnp.zeros_like(zdn)

    for c in range(chunks):
        @pl.when(d > 0)
        def _():
            down_copy(c).wait_recv()

        def one(i, _):
            n = c * step + i
            xg[0, p * pairs + n] = (src[n] + coup[n] * zdn[n].astype(F32)).astype(BF16)
            return 0

        lax.fori_loop(0, step, one, 0, unroll=True)
        push(0, c)

    lanes = lax.broadcasted_iota(jnp.int32, (PATCH_DEV, onehot.shape[1]), 0)
    onehot[...] = jnp.where(lanes == patch[...] % PATCH_DEV, 1.0, 0.0).astype(BF16)

    collect(0)

    def down_chunk(c, _):
        load(c).wait()

        def one(i, _):
            n = c * step + 2 * i
            lower, upper = product(c * (step // 2) + i)
            swept[n] = lower.astype(BF16)
            swept[n + 1] = upper.astype(BF16)
            return 0

        lax.fori_loop(0, step // 2, one, 0)

        @pl.when(d < depths - 1)
        def _():
            down_copy(c).start()

        @pl.when(d == depths - 1)
        def _():
            def keep(i, _):
                pre[c * step + i] = swept[c * step + i]
                return 0

            lax.fori_loop(0, step, keep, 0)
            send_up(c)

        return 0

    lax.fori_loop(0, chunks, down_chunk, 0)

    @pl.when(d < depths - 1)
    def _():
        for c in range(chunks):
            up_copy(c).wait_recv()
            push(1, c)
        collect(1)

        def up_chunk(c, _):
            def one(i, _):
                n = c * step + 2 * i
                lower, upper = product(c * (step // 2) + i)
                pre[n] = (swept[n].astype(F32) + lower).astype(BF16)
                pre[n + 1] = (swept[n + 1].astype(F32) + upper).astype(BF16)
                return 0

            lax.fori_loop(0, step // 2, one, 0)
            send_up(c)
            return 0

        lax.fori_loop(0, chunks, up_chunk, 0)

    terms = []
    for i in range(pairs):
        both = pre[i].astype(F32) * toar[i].astype(F32)
        terms.append(both[:vecs] + both[vecs:])
    contrib = jnp.concatenate(terms, 1)
    named = jnp.broadcast_to(patch[...] // PATCH_DEV, contrib.shape)

    def mask(h, _):
        lhs[h] = jnp.concatenate(
            [jnp.where(named == 2 * h, contrib, 0.0), jnp.where(named == 2 * h + 1, contrib, 0.0)],
            0).astype(BF16)
        return 0

    lax.fori_loop(0, owners // 2, mask, 0)
    part[...] = lax.dot_general(
        lhs[...].reshape(owners * vecs, lhs.shape[2]), onehot[...], (((1,), (1,)), ((), ())),
        preferred_element_type=F32).reshape(owners, vecs, PATCH_DEV)

    def first(o):
        t = lax.rem(d + o, depths)
        return remote(part.at[pl.ds(t * planes, planes)], r1.at[o - 1], as_.at[o - 1], ar.at[o - 1], (t, p))

    for o in range(1, depths):
        first(o).start()
    total = part[pl.ds(d * planes, planes)]
    for o in range(1, depths):
        first(o).wait_recv()
        total = total + r1[o - 1]
    s1[...] = total

    def second(o):
        t = lax.rem(p + o, planes)
        return remote(s1.at[t], r2.at[o - 1], bs.at[o - 1], br.at[o - 1], (d, t))

    for o in range(1, planes):
        second(o).start()
    last = s1[p]
    for o in range(1, planes):
        second(o).wait_recv()
        last = last + r2[o - 1]
    owned[...] = last

    sent(0)

    @pl.when(d < depths - 1)
    def _():
        sent(1)
        for c in range(chunks):
            down_copy(c).wait_send()

    @pl.when(d > 0)
    def _():
        for c in range(chunks):
            up_copy(c).wait_send()

    for o in range(1, depths):
        first(o).wait_send()
    for o in range(1, planes):
        second(o).wait_send()


def shards(toar, pml_coeff, coupling, inverse, pattern, patch_map):
    depths, planes = lax.axis_size("depth"), lax.axis_size("plane")
    _, vecs, _, cells = toar.shape
    block_rows, per_row, blk = inverse.shape[1:4]
    pairs = cells // 128
    owners = depths * planes

    def tiles(value):
        return value.reshape(2 * vecs, pairs, 128).transpose(1, 0, 2)

    vectors = toar[0].transpose(1, 0, 2)
    wide = vectors.astype(F32)
    coeff = pml_coeff[0][:, None]
    source = jnp.concatenate(
        [coeff[0] * wide[0] - coeff[1] * wide[1], coeff[0] * wide[1] + coeff[1] * wide[0]], 0)
    tile = (pairs, 2 * vecs, 128)
    vmem = pl.BlockSpec(memory_space=pltpu.VMEM)
    dma = pltpu.SemaphoreType.DMA
    pre, owned = pl.pallas_call(
        functools.partial(sweep_kernel, depths, planes, pairs, CHUNKS, per_row, vecs),
        out_shape=(jax.ShapeDtypeStruct(tile, BF16), jax.ShapeDtypeStruct((vecs, PATCH_DEV), F32)),
        in_specs=[pl.BlockSpec(memory_space=pltpu.SMEM)] + [vmem] * 4 + [pl.BlockSpec(memory_space=pl.ANY)],
        out_specs=(vmem, vmem),
        scratch_shapes=[
            pltpu.VMEM((block_rows, per_row, blk, 2 * blk), BF16),
            pltpu.VMEM((2, planes * pairs, 2 * vecs, 128), BF16),
            pltpu.VMEM((planes * block_rows, 2 * vecs, 128), BF16),
            pltpu.VMEM(tile, BF16),
            pltpu.VMEM(tile, BF16),
            pltpu.VMEM(tile, BF16),
            pltpu.VMEM((owners // 2, 2 * vecs, cells), BF16),
            pltpu.VMEM((PATCH_DEV, cells), BF16),
            pltpu.VMEM((owners, vecs, PATCH_DEV), F32),
            pltpu.VMEM((depths - 1, planes, vecs, PATCH_DEV), F32),
            pltpu.VMEM((planes, vecs, PATCH_DEV), F32),
            pltpu.VMEM((planes - 1, vecs, PATCH_DEV), F32),
            dma((CHUNKS,)),
            dma((2, planes - 1, CHUNKS)),
            dma((2, planes - 1, CHUNKS)),
            dma((CHUNKS,)),
            dma((CHUNKS,)),
            dma((CHUNKS,)),
            dma((CHUNKS,)),
            dma((depths - 1,)),
            dma((depths - 1,)),
            dma((planes - 1,)),
            dma((planes - 1,)),
        ],
        compiler_params=pltpu.CompilerParams(
            collective_id=0, has_side_effects=True, vmem_limit_bytes=56 * 1024 * 1024),
        cost_estimate=pl.CostEstimate(
            flops=4 * block_rows * per_row * blk * 2 * blk * 2 * vecs,
            bytes_accessed=2 * block_rows * per_row * blk * 2 * blk, transcendentals=0),
    )(
        pattern[0].reshape(-1), tiles(source), coupling[0].reshape(pairs, 1, 128),
        tiles(vectors), patch_map, inverse[0],
    )
    precond = pre.transpose(1, 0, 2).reshape(2, vecs, cells).transpose(1, 0, 2)
    return (precond[None], owned)


def solution(mesh):
    return jax.shard_map(
        shards,
        mesh=mesh,
        in_specs=(
            P("depth", None, None, "plane"),
            P("depth", None, "plane"),
            P("depth", "plane"),
            P("depth", "plane", None, None, None),
            P("depth", "plane", None),
            P("depth", "plane"),
        ),
        out_specs=(P("depth", None, None, "plane"), P(None, ("depth", "plane"))),
        check_vma=False,
    )
```
